768 devices in a mesh: section: 16 (over y_lo, x), expert: 48 (over z, y_hi, core).
Axes of the slice: x: 4, y: 8 (y_hi: 2, y_lo: 4; y = y_hi * 4 + y_lo), z: 12, core: 2. Of those that a mesh axis runs over, the one named last changes fastest.
Arguments:
- fwd_held: bfloat16 [16, 3072, 3584], P('section', 'expert'), may hold values from -6 to 6
- saved_preact: bfloat16 [16, 48, 2, 2, 6144], P('section', None, None, None, 'expert'), may hold values from -6 to 6
- grad_held: bfloat16 [16, 3072, 3584], P('section', 'expert'), may hold values from -6 to 6
- gate_weight: bfloat16 [16, 3584, 6144], P('section', None, 'expert'), may hold values from -0.09375 to 0.09375
- up_weight: bfloat16 [16, 3584, 6144], P('section', None, 'expert'), may hold values from -0.09375 to 0.09375
- down_weight: bfloat16 [16, 6144, 3584], P('section', 'expert'), may hold values from -0.125 to 0.125
- fwd_slots: int32 [16, 48, 3, 2], P('section', 'expert'), may hold values from 0 to 64, as said below
- fwd_gates: float32 [16, 48, 3, 2], P('section', 'expert'), may hold values from 0.2 to 1
- bwd_slots: int32 [16, 48, 3, 2], P('section', 'expert'), may hold values from 0 to 64, as said below
- bwd_gates: float32 [16, 48, 3, 2], P('section', 'expert'), may hold values from 0.2 to 1
Outputs:
- fwd_out: bfloat16 [16, 3072, 3584], P('section', 'expert')
- grad_out: bfloat16 [16, 3072, 3584], P('section', 'expert')
The draws below stay inside these ranges and needn't reach their ends.
Inputs may be any that keep to these rules, and one draw needn't show every extreme that they name: `fwd_slots`: each entry names a token of the same device's block of 64 tokens, or 64 for an empty slot; the filled slots of one section, device and expert name distinct tokens. `bwd_slots`: each entry names a token of the same device's block of 64 tokens, or 64 for an empty slot; the filled slots of one section, device and expert name distinct tokens.
All inputs are finite; a program needn't handle non-finite values.
Results may differ from the reference program's by a relative error of at most 0.0023.
Values may be sent and summed in bfloat16 or wider, within the bound.
No kernel may reach another device: no remote copies, remote signals or barrier semaphores. Data moves between devices by JAX's collectives and lax.ppermute only.
A program may use at most 32 MiB of HBM per device.

```python
import math
import jax
import jax.numpy as jnp
from jax import lax

D = 3584
EFF = 2048
TOK_DEV = 64
CAP = 2
SPLIT = 16
GROUPS = 3
FF_DEV = 128
TOKENS = 3072
N_SECTION = 16
N_EXPERT = 48


def make_slots(key):
    keys = jax.random.split(key, 2)
    shape = (N_SECTION, N_EXPERT, GROUPS, TOK_DEV)
    scores = jax.random.randint(keys[0], shape, 0, 1 << 20) * TOK_DEV + jnp.arange(TOK_DEV, dtype=jnp.int32)
    order = jnp.argsort(scores, axis=-1)[..., :CAP].astype(jnp.int32)
    empty = jax.random.randint(keys[1], order.shape, 0, 4) == 0
    return jnp.where(empty, TOK_DEV, order).astype(jnp.int32)


def draw_fwd_slots(key, part):
    key = jax.random.fold_in(key, 11)
    return make_slots(key)


def draw_bwd_slots(key, part):
    key = jax.random.fold_in(key, 23)
    return make_slots(key)


def shard_levels(rng, extent, cuts, least, top_value):
    def one(dim, blocks):
        heights = jax.random.uniform(jax.random.fold_in(jax.random.fold_in(rng, 6), dim), (blocks,), jnp.float32, least / len(cuts), top_value / len(cuts))
        return jnp.repeat(jnp.exp(heights), extent[dim] // blocks).reshape((-1,) + (1,) * (len(extent) - dim - 1))

    loudness = one(*cuts[0])
    for cut in cuts[1:]:
        loudness = loudness * one(*cut)
    return loudness


def gaussian(own_key, shape, scale, bound, shards=(), kind=jnp.bfloat16):
    array = jax.random.normal(own_key, shape, jnp.float32) * scale
    if len(shards) > 0:
        array = shard_levels(own_key, shape, shards, -0.22, 0.18) * array
    return jnp.clip(array, min=-bound, max=bound).astype(kind)


def setup_inputs(seed: int = 0) -> dict:
    arg_keys = jax.random.split(jax.random.key(seed), 11)
    return {
        "fwd_held": gaussian(arg_keys[0], (N_SECTION, TOKENS, D), 1.0, 6.0, ((0, 16), (1, 48))),
        "saved_preact": gaussian(arg_keys[1], (N_SECTION, N_EXPERT, CAP, 2, GROUPS * EFF), 1.5, 6.0, ((0, 16), (4, 48))),
        "grad_held": gaussian(arg_keys[2], (N_SECTION, TOKENS, D), 1.0, 6.0, ((0, 16), (1, 48))),
        "gate_weight": gaussian(arg_keys[3], (N_SECTION, D, GROUPS * EFF), D ** -0.5, 0.09375, ((0, 16), (2, 48))),
        "up_weight": gaussian(arg_keys[4], (N_SECTION, D, GROUPS * EFF), D ** -0.5, 0.09375, ((0, 16), (2, 48))),
        "down_weight": gaussian(arg_keys[5], (N_SECTION, GROUPS * EFF, D), EFF ** -0.5, 0.125, ((0, 16), (1, 48))),
        "fwd_slots": draw_fwd_slots(jax.random.fold_in(arg_keys[10], 71), 0),
        "fwd_gates": jnp.clip(jnp.exp(math.log(1.0) - 1.609438 * jax.random.uniform(arg_keys[7], (N_SECTION, N_EXPERT, GROUPS, CAP), jnp.float32) ** shard_levels(arg_keys[7], (N_SECTION, N_EXPERT, GROUPS, CAP), ((0, 16), (1, 48)), -0.2, 0.2)), 0.2, 1.0),
        "bwd_slots": draw_bwd_slots(jax.random.fold_in(arg_keys[10], 71), 0),
        "bwd_gates": jnp.clip(jnp.exp(math.log(1.0) - 1.609438 * jax.random.uniform(arg_keys[9], (N_SECTION, N_EXPERT, GROUPS, CAP), jnp.float32) ** shard_levels(arg_keys[9], (N_SECTION, N_EXPERT, GROUPS, CAP), ((0, 16), (1, 48)), -0.2, 0.2)), 0.2, 1.0),
    }


def take_rows(block, slots):
    padded = jnp.concatenate([block, jnp.zeros((N_EXPERT, 1, D), block.dtype)], axis=1)
    index = slots.reshape(N_EXPERT, GROUPS * CAP).astype(jnp.int32)
    rows = jnp.take_along_axis(padded, index[:, :, None], axis=1)
    return rows.reshape(N_EXPERT, GROUPS, CAP, D)


def combine(block, slots, gates, result):
    onehot = (slots[..., None] == jnp.arange(TOK_DEV, dtype=jnp.int32)).astype(jnp.float32)
    weighted = onehot * gates[..., None]
    added = jnp.einsum("egct,egcd->etd", weighted, result, precision=lax.Precision.HIGHEST)
    return (block.astype(jnp.float32) + added).astype(jnp.bfloat16)


def reference(fwd_held, saved_preact, grad_held, gate_weight, up_weight, down_weight, fwd_slots, fwd_gates, bwd_slots, bwd_gates):
    high = lax.Precision.HIGHEST
    fwd_list = []
    grad_list = []
    for section in range(N_SECTION):
        w_gate = gate_weight[section].astype(jnp.float32)
        w_up = up_weight[section].astype(jnp.float32)
        w_down = down_weight[section].astype(jnp.float32)
        inputs = fwd_held[(section - 1) % N_SECTION]
        block = inputs.reshape(N_EXPERT, TOK_DEV, D)
        rows = take_rows(block, fwd_slots[section]).astype(jnp.float32)
        pre_gate = jnp.einsum("egcd,dgf->egcf", rows, w_gate.reshape(D, GROUPS, EFF), precision=high)
        pre_up = jnp.einsum("egcd,dgf->egcf", rows, w_up.reshape(D, GROUPS, EFF), precision=high)
        hidden = (jax.nn.silu(pre_gate) * pre_up).astype(jnp.bfloat16).astype(jnp.float32)
        hidden = hidden.reshape(N_EXPERT, GROUPS, CAP, SPLIT, FF_DEV)
        parts = jnp.einsum("egcsf,gsfd->egcsd", hidden, w_down.reshape(GROUPS, SPLIT, FF_DEV, D), precision=high)
        parts = lax.optimization_barrier(parts.astype(jnp.bfloat16)).astype(jnp.float32)
        expert_out = jnp.sum(parts, axis=3)
        fwd_list.append(combine(block, fwd_slots[section], fwd_gates[section], expert_out).reshape(TOKENS, D))

        incoming = grad_held[(section + 1) % N_SECTION]
        gblock = incoming.reshape(N_EXPERT, TOK_DEV, D)
        grows = take_rows(gblock, bwd_slots[section]).astype(jnp.float32)
        saved = saved_preact[section].astype(jnp.float32)
        pre_a = saved[:, :, 0, :].reshape(N_EXPERT, CAP, GROUPS, EFF).transpose(0, 2, 1, 3)
        pre_v = saved[:, :, 1, :].reshape(N_EXPERT, CAP, GROUPS, EFF).transpose(0, 2, 1, 3)
        dh = jnp.einsum("egcd,gfd->egcf", grows, w_down.reshape(GROUPS, EFF, D), precision=high)
        sig = jax.nn.sigmoid(pre_a)
        act = pre_a * sig
        slope = sig * (1.0 + pre_a * (1.0 - sig))
        d_gate = (dh * pre_v * slope).astype(jnp.bfloat16).astype(jnp.float32)
        d_up = (dh * act).astype(jnp.bfloat16).astype(jnp.float32)
        d_gate = d_gate.reshape(N_EXPERT, GROUPS, CAP, SPLIT, FF_DEV)
        d_up = d_up.reshape(N_EXPERT, GROUPS, CAP, SPLIT, FF_DEV)
        gparts = jnp.einsum("egcsf,dgsf->egcsd", d_gate, w_gate.reshape(D, GROUPS, SPLIT, FF_DEV), precision=high)
        gparts = gparts + jnp.einsum("egcsf,dgsf->egcsd", d_up, w_up.reshape(D, GROUPS, SPLIT, FF_DEV), precision=high)
        gparts = lax.optimization_barrier(gparts.astype(jnp.bfloat16)).astype(jnp.float32)
        expert_grad = jnp.sum(gparts, axis=3)
        grad_list.append(combine(gblock, bwd_slots[section], bwd_gates[section], expert_grad).reshape(TOKENS, D))
    return jnp.stack(fwd_list), jnp.stack(grad_list)
```

```python
import jax
import jax.numpy as jnp
from jax import lax
from jax.sharding import PartitionSpec as P

CORES = 2
HALVES = 2
GROUPS = 3


def shifted(shard, axis, by):
    length = lax.axis_size(axis)
    return lax.ppermute(shard, axis, [(i, (i + by) % length) for i in range(length)])


def layout(length):
    depth = length // (GROUPS * HALVES * CORES)

    def at(group, z, half, core):
        return ((group * depth + z) * HALVES + half) * CORES + core

    zs, halves, cores, groups = range(depth), range(HALVES), range(CORES), range(GROUPS)
    far = [[at(g, z, h, c) for g in groups for h in halves] for z in zs for c in cores]
    line = [[at(g, z, h, c) for z in zs] for g in groups for h in halves for c in cores]
    pair = [[at(g, z, h, c) for c in cores] for g in groups for z in zs for h in halves]
    return depth, far, line, pair


def pick_rows(slots, block):
    count = block.shape[0]
    flat = slots.reshape(-1)
    onehot = flat[:, None] == jnp.arange(count, dtype=jnp.int32)[None, :]
    rows = jnp.dot(onehot.astype(jnp.bfloat16), block, preferred_element_type=jnp.float32).astype(
        jnp.bfloat16
    )
    return (onehot.astype(jnp.float32), rows)


def settle(result, onehot, gates, block):
    weighted = onehot * gates.reshape(-1)[:, None]
    added = lax.dot_general(
        weighted, result, (((0,), (0,)), ((), ())), precision=lax.Precision.HIGHEST
    )
    return (block.astype(jnp.float32) + added).astype(jnp.bfloat16)


def local(
    fwd_held,
    saved_preact,
    grad_held,
    gate_weight,
    up_weight,
    down_weight,
    fwd_slots,
    fwd_gates,
    bwd_slots,
    bwd_gates,
):
    width = fwd_held.shape[2]
    cap = fwd_slots.shape[3]
    both = 2 * cap
    length = lax.axis_size("expert")
    depth, far, line, pair = layout(length)
    spokes = GROUPS * HALVES
    w_gate = gate_weight[0]
    w_up = up_weight[0]
    w_down = down_weight[0]
    hidden_width = w_down.shape[0]

    inputs = shifted(fwd_held, "section", 1)[0]
    incoming = shifted(grad_held, "section", -1)[0]

    saved = saved_preact[0].reshape(GROUPS, depth, HALVES, CORES, cap, 2, hidden_width)
    saved = saved.transpose(5, 3, 1, 0, 2, 4, 6)
    saved = jnp.concatenate([jnp.zeros_like(saved), saved], axis=5)
    saved = saved.reshape(2, -1, hidden_width).astype(jnp.float32)
    pre_a, pre_v = saved[0], saved[1]

    fwd_hot, fwd_rows = pick_rows(fwd_slots[0, 0], inputs)
    bwd_hot, bwd_rows = pick_rows(bwd_slots[0, 0], incoming)
    rows = jnp.concatenate(
        [fwd_rows.reshape(GROUPS, cap, width), bwd_rows.reshape(GROUPS, cap, width)], axis=1
    )
    rows = jnp.broadcast_to(rows[:, None], (GROUPS, HALVES, both, width)).reshape(spokes, both, width)
    rows = lax.all_to_all(rows, "expert", 0, 0, axis_index_groups=far, tiled=True)
    rows = rows.reshape(spokes * both, width)
    rows = lax.all_gather(rows, "expert", axis_index_groups=line, tiled=True)
    rows = lax.all_gather(rows, "expert", axis_index_groups=pair, tiled=True)

    pre_gate = jnp.dot(rows, w_gate, preferred_element_type=jnp.float32)
    pre_up = jnp.dot(rows, w_up, preferred_element_type=jnp.float32)
    dh = lax.dot_general(rows, w_down, (((1,), (1,)), ((), ())), preferred_element_type=jnp.float32)
    is_fwd = (lax.broadcasted_iota(jnp.int32, pre_gate.shape, 0) % both) < cap
    hidden = jnp.where(is_fwd, jax.nn.silu(pre_gate) * pre_up, 0.0)
    sig = jax.nn.sigmoid(pre_a)
    act = pre_a * sig
    slope = sig * (1.0 + pre_a * (1.0 - sig))
    acts = jnp.concatenate([hidden, dh * pre_v * slope, dh * act], axis=1).astype(jnp.bfloat16)
    w_out = jnp.concatenate([w_down, w_gate.T, w_up.T], axis=0)
    part = jnp.dot(acts, w_out, preferred_element_type=jnp.float32).astype(jnp.bfloat16)

    def summed(parts, members, groups):
        parts = parts.reshape(members, -1, width)
        parts = lax.all_to_all(parts, "expert", 0, 0, axis_index_groups=groups, tiled=True)
        return parts.astype(jnp.float32).sum(axis=0).astype(jnp.bfloat16)

    part = summed(part, CORES, pair)
    part = summed(part, depth, line)
    part = part.reshape(spokes, both, width)
    part = lax.all_to_all(part, "expert", 0, 0, axis_index_groups=far, tiled=True)
    part = part.astype(jnp.float32).reshape(GROUPS, HALVES, both, width).sum(axis=1)
    fwd_out = settle(part[:, :cap].reshape(-1, width), fwd_hot, fwd_gates[0, 0], inputs)
    grad_out = settle(part[:, cap:].reshape(-1, width), bwd_hot, bwd_gates[0, 0], incoming)
    return (fwd_out[None], grad_out[None])


def solution(mesh):
    in_specs = (
        P("section", "expert", None),
        P("section", None, None, None, "expert"),
        P("section", "expert", None),
        P("section", None, "expert"),
        P("section", None, "expert"),
        P("section", "expert", None),
        P("section", "expert", None, None),
        P("section", "expert", None, None),
        P("section", "expert", None, None),
        P("section", "expert", None, None),
    )
    out_specs = (P("section", "expert", None), P("section", "expert", None))
    return jax.shard_map(local, mesh=mesh, in_specs=in_specs, out_specs=out_specs, check_vma=False)
```

```python
import jax
import jax.numpy as jnp
from jax import lax
from jax.sharding import PartitionSpec as P

CORES = 2
GROUPS = 3


def shifted(shard, axis, by):
    length = lax.axis_size(axis)
    return lax.ppermute(shard, axis, [(i, (i + by) % length) for i in range(length)])


def swapped(shard, axis):
    length = lax.axis_size(axis)
    return lax.ppermute(shard, axis, [(i, i ^ 1) for i in range(length)])


def pick_rows(slots, block):
    count = block.shape[0]
    flat = slots.reshape(-1)
    onehot = flat[:, None] == jnp.arange(count, dtype=jnp.int32)[None, :]
    rows = jnp.dot(onehot.astype(jnp.bfloat16), block, preferred_element_type=jnp.float32).astype(
        jnp.bfloat16
    )
    return (onehot.astype(jnp.float32), rows)


def settle(result, onehot, gates, block):
    weighted = onehot * gates.reshape(-1)[:, None]
    added = lax.dot_general(
        weighted, result, (((0,), (0,)), ((), ())), precision=lax.Precision.HIGHEST
    )
    return (block.astype(jnp.float32) + added).astype(jnp.bfloat16)


def local(
    fwd_held,
    saved_preact,
    grad_held,
    gate_weight,
    up_weight,
    down_weight,
    fwd_slots,
    fwd_gates,
    bwd_slots,
    bwd_gates,
):
    width = fwd_held.shape[2]
    cap = fwd_slots.shape[3]
    both = 2 * cap
    length = lax.axis_size("expert")
    chips = length // CORES
    same_core = [[chip * CORES + core for chip in range(chips)] for core in range(CORES)]
    core = lax.axis_index("expert") % CORES
    w_gate = gate_weight[0]
    w_up = up_weight[0]
    w_down = down_weight[0]
    hidden_width = w_down.shape[0]

    inputs = shifted(fwd_held, "section", 1)[0]
    incoming = shifted(grad_held, "section", -1)[0]

    saved = saved_preact[0].reshape(chips, CORES, cap, 2, hidden_width)

    def saved_of(which):
        part = lax.dynamic_index_in_dim(saved, which, 1, keepdims=False)
        part = jnp.concatenate([jnp.zeros_like(part), part], axis=1)
        part = part.transpose(2, 0, 1, 3).reshape(2, -1, hidden_width).astype(jnp.float32)
        return part[0], part[1]

    fwd_hot, fwd_rows = pick_rows(fwd_slots[0, 0], inputs)
    bwd_hot, bwd_rows = pick_rows(bwd_slots[0, 0], incoming)
    rows = jnp.concatenate(
        [fwd_rows.reshape(GROUPS, cap, width), bwd_rows.reshape(GROUPS, cap, width)], axis=1
    )
    rows = jnp.broadcast_to(rows[:, None], (GROUPS, chips // GROUPS, both, width))
    rows = rows.reshape(chips, both, width)
    rows = lax.all_to_all(rows, "expert", 0, 0, axis_index_groups=same_core, tiled=True)
    mine = rows.reshape(chips * both, width)
    other = swapped(mine, "expert")

    def expert(rows, pre_a, pre_v):
        pre_gate = jnp.dot(rows, w_gate, preferred_element_type=jnp.float32)
        pre_up = jnp.dot(rows, w_up, preferred_element_type=jnp.float32)
        dh = lax.dot_general(rows, w_down, (((1,), (1,)), ((), ())), preferred_element_type=jnp.float32)
        is_fwd = (lax.broadcasted_iota(jnp.int32, pre_gate.shape, 0) % both) < cap
        hidden = jnp.where(is_fwd, jax.nn.silu(pre_gate) * pre_up, 0.0)
        sig = jax.nn.sigmoid(pre_a)
        act = pre_a * sig
        slope = sig * (1.0 + pre_a * (1.0 - sig))
        acts = jnp.concatenate([hidden, dh * pre_v * slope, dh * act], axis=1).astype(jnp.bfloat16)
        w_out = jnp.concatenate([w_down, w_gate.T, w_up.T], axis=0)
        return jnp.dot(acts, w_out, preferred_element_type=jnp.float32).astype(jnp.bfloat16)

    away = swapped(expert(other, *saved_of(1 - core)), "expert")
    home = expert(mine, *saved_of(core))
    part = (home.astype(jnp.float32) + away.astype(jnp.float32)).astype(jnp.bfloat16)
    part = part.reshape(chips, both, width)
    part = lax.all_to_all(part, "expert", 0, 0, axis_index_groups=same_core, tiled=True)
    part = part.astype(jnp.float32).reshape(GROUPS, chips // GROUPS, both, width).sum(axis=1)
    fwd_out = settle(part[:, :cap].reshape(-1, width), fwd_hot, fwd_gates[0, 0], inputs)
    grad_out = settle(part[:, cap:].reshape(-1, width), bwd_hot, bwd_gates[0, 0], incoming)
    return (fwd_out[None], grad_out[None])


def solution(mesh):
    in_specs = (
        P("section", "expert", None),
        P("section", None, None, None, "expert"),
        P("section", "expert", None),
        P("section", None, "expert"),
        P("section", None, "expert"),
        P("section", "expert", None),
        P("section", "expert", None, None),
        P("section", "expert", None, None),
        P("section", "expert", None, None),
        P("section", "expert", None, None),
    )
    out_specs = (P("section", "expert", None), P("section", "expert", None))
    return jax.shard_map(local, mesh=mesh, in_specs=in_specs, out_specs=out_specs, check_vma=False)
```

```python
import jax
import jax.numpy as jnp
from jax import lax
from jax.experimental import pallas as pl
from jax.experimental.pallas import tpu as pltpu
from jax.sharding import PartitionSpec as P

CORES = 2
GROUPS = 3


def shifted(shard, axis, by):
    length = lax.axis_size(axis)
    return lax.ppermute(shard, axis, [(i, (i + by) % length) for i in range(length)])


def swapped(shard, axis):
    length = lax.axis_size(axis)
    return lax.ppermute(shard, axis, [(i, i ^ 1) for i in range(length)])


def pick_rows(slots, block):
    onehot = slots[:, None] == jnp.arange(block.shape[0], dtype=jnp.int32)[None, :]
    return jnp.dot(onehot.astype(jnp.bfloat16), block, preferred_element_type=jnp.float32).astype(
        jnp.bfloat16
    )


def settle_kernel(
    fwd_slots, fwd_gates, bwd_slots, bwd_gates, back, inputs, incoming, fwd_out, grad_out, total
):
    chips, both, _ = back.shape
    cap = both // 2
    pieces = chips // GROUPS
    tokens = inputs.shape[0]
    sums = []
    for group in range(GROUPS):
        acc = back[group * pieces].astype(jnp.float32)
        for piece in range(1, pieces):
            acc = acc + back[group * pieces + piece].astype(jnp.float32)
        sums.append(acc)
    jobs = ((fwd_slots, fwd_gates, inputs, fwd_out, 0), (bwd_slots, bwd_gates, incoming, grad_out, cap))
    for slots, gates, block, out, first in jobs:
        total[:tokens] = block[...].astype(jnp.float32)
        for group in range(GROUPS):
            for slot in range(cap):
                row = pl.ds(slots[group * cap + slot], 1)
                piece = sums[group][first + slot : first + slot + 1]
                total[row] = total[row] + gates[group * cap + slot] * piece
        out[...] = total[:tokens].astype(out.dtype)


def settle(back, fwd_slots, fwd_gates, inputs, bwd_slots, bwd_gates, incoming):
    chips, both, width = back.shape
    tokens = inputs.shape[0]
    step = width // 4
    smem = pl.BlockSpec(memory_space=pltpu.SMEM)
    rows = pl.BlockSpec((tokens, step), lambda i: (0, i))
    return pl.pallas_call(
        settle_kernel,
        grid=(width // step,),
        out_shape=[jax.ShapeDtypeStruct((tokens, width), jnp.bfloat16)] * 2,
        in_specs=[smem] * 4 + [pl.BlockSpec((chips, both, step), lambda i: (0, 0, i)), rows, rows],
        out_specs=[rows, rows],
        scratch_shapes=[pltpu.VMEM((tokens + 8, step), jnp.float32)],
        compiler_params=pltpu.CompilerParams(vmem_limit_bytes=16 * 1024 * 1024),
        cost_estimate=pl.CostEstimate(flops=2 * chips * both * width, bytes_accessed=2560 * width // 4, transcendentals=0),
        name="settle",
    )(fwd_slots, fwd_gates, bwd_slots, bwd_gates, back, inputs, incoming)


def local(
    fwd_held,
    saved_preact,
    grad_held,
    gate_weight,
    up_weight,
    down_weight,
    fwd_slots,
    fwd_gates,
    bwd_slots,
    bwd_gates,
):
    width = fwd_held.shape[2]
    cap = fwd_slots.shape[3]
    both = 2 * cap
    length = lax.axis_size("expert")
    chips = length // CORES
    same_core = [[chip * CORES + core for chip in range(chips)] for core in range(CORES)]
    core = lax.axis_index("expert") % CORES
    w_gate = gate_weight[0]
    w_up = up_weight[0]
    w_down = down_weight[0]
    hidden_width = w_down.shape[0]

    inputs = shifted(fwd_held, "section", 1)[0]
    incoming = shifted(grad_held, "section", -1)[0]
    fwd_index = fwd_slots.reshape(-1)
    bwd_index = bwd_slots.reshape(-1)

    saved = saved_preact[0].reshape(chips, CORES, cap, 2, hidden_width)

    def saved_of(which):
        part = lax.dynamic_index_in_dim(saved, which, 1, keepdims=False)
        part = jnp.concatenate([jnp.zeros_like(part), part], axis=1)
        part = part.transpose(2, 0, 1, 3).reshape(2, -1, hidden_width).astype(jnp.float32)
        return part[0], part[1]

    saves = (*saved_of(core), *saved_of(1 - core))
    w_out = jnp.concatenate([w_down, w_gate.T, w_up.T], axis=0)

    fwd_rows = pick_rows(fwd_index, inputs)
    bwd_rows = pick_rows(bwd_index, incoming)
    rows = jnp.concatenate(
        [fwd_rows.reshape(GROUPS, cap, width), bwd_rows.reshape(GROUPS, cap, width)], axis=1
    )
    rows = jnp.broadcast_to(rows[:, None], (GROUPS, chips // GROUPS, both, width))
    rows = rows.reshape(chips, both, width)
    rows, w_out, saves = lax.optimization_barrier((rows, w_out, saves))
    rows = lax.all_to_all(rows, "expert", 0, 0, axis_index_groups=same_core, tiled=True)
    mine = rows.reshape(chips * both, width)
    other = swapped(mine, "expert")

    def expert(rows, pre_a, pre_v):
        pre_gate = jnp.dot(rows, w_gate, preferred_element_type=jnp.float32)
        pre_up = jnp.dot(rows, w_up, preferred_element_type=jnp.float32)
        dh = lax.dot_general(rows, w_down, (((1,), (1,)), ((), ())), preferred_element_type=jnp.float32)
        is_fwd = (lax.broadcasted_iota(jnp.int32, pre_gate.shape, 0) % both) < cap
        hidden = jnp.where(is_fwd, jax.nn.silu(pre_gate) * pre_up, 0.0)
        sig = jax.nn.sigmoid(pre_a)
        act = pre_a * sig
        slope = sig * (1.0 + pre_a * (1.0 - sig))
        acts = jnp.concatenate([hidden, dh * pre_v * slope, dh * act], axis=1).astype(jnp.bfloat16)
        return jnp.dot(acts, w_out, preferred_element_type=jnp.float32).astype(jnp.bfloat16)

    away = swapped(expert(other, *saves[2:]), "expert")
    home = expert(mine, *saves[:2])
    part = (home.astype(jnp.float32) + away.astype(jnp.float32)).astype(jnp.bfloat16)
    part = part.reshape(chips, both, width)
    part = lax.all_to_all(part, "expert", 0, 0, axis_index_groups=same_core, tiled=True)
    fwd_out, grad_out = settle(
        part, fwd_index, fwd_gates.reshape(-1), inputs, bwd_index, bwd_gates.reshape(-1), incoming
    )
    return (fwd_out[None], grad_out[None])


def solution(mesh):
    in_specs = (
        P("section", "expert", None),
        P("section", None, None, None, "expert"),
        P("section", "expert", None),
        P("section", None, "expert"),
        P("section", None, "expert"),
        P("section", "expert", None),
        P("section", "expert", None, None),
        P("section", "expert", None, None),
        P("section", "expert", None, None),
        P("section", "expert", None, None),
    )
    out_specs = (P("section", "expert", None), P("section", "expert", None))
    return jax.shard_map(local, mesh=mesh, in_specs=in_specs, out_specs=out_specs, check_vma=False)
```

```python
import jax
import jax.numpy as jnp
from jax import lax
from jax.experimental import pallas as pl
from jax.experimental.pallas import tpu as pltpu
from jax.sharding import PartitionSpec as P

CORES = 2
GROUPS = 3


def shifted(shard, axis, by):
    length = lax.axis_size(axis)
    return lax.ppermute(shard, axis, [(i, (i + by) % length) for i in range(length)])


def swapped(shard, axis):
    length = lax.axis_size(axis)
    return lax.ppermute(shard, axis, [(i, i ^ 1) for i in range(length)])


def pick_rows(slots, block):
    onehot = slots[:, None] == jnp.arange(block.shape[0], dtype=jnp.int32)[None, :]
    return jnp.dot(onehot.astype(jnp.bfloat16), block, preferred_element_type=jnp.float32).astype(
        jnp.bfloat16
    )


def settle_kernel(
    fwd_slots, fwd_gates, bwd_slots, bwd_gates, back, inputs, incoming, fwd_out, grad_out, total
):
    chips, both, _ = back.shape
    cap = both // 2
    pieces = chips // GROUPS
    tokens = inputs.shape[0]
    sums = []
    for group in range(GROUPS):
        acc = back[group * pieces].astype(jnp.float32)
        for piece in range(1, pieces):
            acc = acc + back[group * pieces + piece].astype(jnp.float32)
        sums.append(acc)
    jobs = ((fwd_slots, fwd_gates, inputs, fwd_out, 0), (bwd_slots, bwd_gates, incoming, grad_out, cap))
    for slots, gates, block, out, first in jobs:
        total[:tokens] = block[...].astype(jnp.float32)
        for group in range(GROUPS):
            for slot in range(cap):
                row = pl.ds(slots[group * cap + slot], 1)
                piece = sums[group][first + slot : first + slot + 1]
                total[row] = total[row] + gates[group * cap + slot] * piece
        out[...] = total[:tokens].astype(out.dtype)


def settle(back, fwd_slots, fwd_gates, inputs, bwd_slots, bwd_gates, incoming):
    chips, both, width = back.shape
    tokens = inputs.shape[0]
    step = width // 4
    smem = pl.BlockSpec(memory_space=pltpu.SMEM)
    rows = pl.BlockSpec((tokens, step), lambda i: (0, i))
    return pl.pallas_call(
        settle_kernel,
        grid=(width // step,),
        out_shape=[jax.ShapeDtypeStruct((tokens, width), jnp.bfloat16)] * 2,
        in_specs=[smem] * 4 + [pl.BlockSpec((chips, both, step), lambda i: (0, 0, i)), rows, rows],
        out_specs=[rows, rows],
        scratch_shapes=[pltpu.VMEM((tokens + 8, step), jnp.float32)],
        compiler_params=pltpu.CompilerParams(vmem_limit_bytes=16 * 1024 * 1024),
        cost_estimate=pl.CostEstimate(flops=2 * chips * both * width, bytes_accessed=2560 * width // 4, transcendentals=0),
        name="settle",
    )(fwd_slots, fwd_gates, bwd_slots, bwd_gates, back, inputs, incoming)


def local(
    fwd_held,
    saved_preact,
    grad_held,
    gate_weight,
    up_weight,
    down_weight,
    fwd_slots,
    fwd_gates,
    bwd_slots,
    bwd_gates,
):
    width = fwd_held.shape[2]
    cap = fwd_slots.shape[3]
    both = 2 * cap
    length = lax.axis_size("expert")
    chips = length // CORES
    same_core = [[chip * CORES + core for chip in range(chips)] for core in range(CORES)]
    core = lax.axis_index("expert") % CORES
    w_gate = gate_weight[0]
    w_up = up_weight[0]
    w_down = down_weight[0]
    hidden_width = w_down.shape[0]

    inputs = shifted(fwd_held, "section", 1)[0]
    incoming = shifted(grad_held, "section", -1)[0]
    fwd_index = fwd_slots.reshape(-1)
    bwd_index = bwd_slots.reshape(-1)

    fwd_rows = pick_rows(fwd_index, inputs)
    bwd_rows = pick_rows(bwd_index, incoming)
    rows = jnp.concatenate(
        [fwd_rows.reshape(GROUPS, cap, width), bwd_rows.reshape(GROUPS, cap, width)], axis=1
    )
    rows = jnp.broadcast_to(rows[:, None], (GROUPS, chips // GROUPS, both, width))
    rows = rows.reshape(chips, both, width)
    rows, w_gate, w_up, saved = lax.optimization_barrier((rows, w_gate, w_up, saved_preact[0]))
    rows = lax.all_to_all(rows, "expert", 0, 0, axis_index_groups=same_core, tiled=True)
    rows = rows.reshape(chips * both, width)

    own = jnp.concatenate([w_down, w_gate.T, w_up.T], axis=0)
    other = swapped(own, "expert")
    saved = saved.reshape(chips, CORES, cap, 2, hidden_width)
    own_saved = lax.dynamic_index_in_dim(saved, core, 1, keepdims=False)
    other_saved = swapped(lax.dynamic_index_in_dim(saved, 1 - core, 1, keepdims=False), "expert")

    def acts_of(weights, saved):
        pre = lax.dot_general(rows, weights, (((1,), (1,)), ((), ())), preferred_element_type=jnp.float32)
        dh, pre_gate, pre_up = jnp.split(pre, 3, axis=1)
        saved = jnp.concatenate([jnp.zeros_like(saved), saved], axis=1)
        saved = saved.transpose(2, 0, 1, 3).reshape(2, -1, hidden_width).astype(jnp.float32)
        pre_a, pre_v = saved[0], saved[1]
        is_fwd = (lax.broadcasted_iota(jnp.int32, pre_gate.shape, 0) % both) < cap
        hidden = jnp.where(is_fwd, jax.nn.silu(pre_gate) * pre_up, 0.0)
        sig = jax.nn.sigmoid(pre_a)
        act = pre_a * sig
        slope = sig * (1.0 + pre_a * (1.0 - sig))
        return jnp.concatenate([hidden, dh * pre_v * slope, dh * act], axis=1).astype(jnp.bfloat16)

    part = jnp.dot(acts_of(own, own_saved), own, preferred_element_type=jnp.float32)
    part = part + jnp.dot(acts_of(other, other_saved), other, preferred_element_type=jnp.float32)
    part = part.astype(jnp.bfloat16).reshape(chips, both, width)
    part = lax.all_to_all(part, "expert", 0, 0, axis_index_groups=same_core, tiled=True)
    fwd_out, grad_out = settle(
        part, fwd_index, fwd_gates.reshape(-1), inputs, bwd_index, bwd_gates.reshape(-1), incoming
    )
    return (fwd_out[None], grad_out[None])


def solution(mesh):
    in_specs = (
        P("section", "expert", None),
        P("section", None, None, None, "expert"),
        P("section", "expert", None),
        P("section", None, "expert"),
        P("section", None, "expert"),
        P("section", "expert", None),
        P("section", "expert", None, None),
        P("section", "expert", None, None),
        P("section", "expert", None, None),
        P("section", "expert", None, None),
    )
    out_specs = (P("section", "expert", None), P("section", "expert", None))
    return jax.shard_map(local, mesh=mesh, in_specs=in_specs, out_specs=out_specs, check_vma=False)
```

```python
import jax
import jax.numpy as jnp
from jax import lax
from jax.experimental import pallas as pl
from jax.experimental.pallas import tpu as pltpu
from jax.sharding import PartitionSpec as P

CORES = 2
GROUPS = 3


def shifted(shard, axis, by):
    length = lax.axis_size(axis)
    return lax.ppermute(shard, axis, [(i, (i + by) % length) for i in range(length)])


def swapped(shard, axis):
    length = lax.axis_size(axis)
    return lax.ppermute(shard, axis, [(i, i ^ 1) for i in range(length)])


def pick_rows(slots, block):
    onehot = slots[:, None] == jnp.arange(block.shape[0], dtype=jnp.int32)[None, :]
    return jnp.dot(onehot.astype(jnp.bfloat16), block, preferred_element_type=jnp.float32).astype(
        jnp.bfloat16
    )


def settle_kernel(
    fwd_slots, fwd_gates, bwd_slots, bwd_gates, back, inputs, incoming, fwd_out, grad_out, total
):
    chips, both, _ = back.shape
    cap = both // 2
    pieces = chips // GROUPS
    tokens = inputs.shape[0]
    sums = []
    for group in range(GROUPS):
        acc = back[group * pieces].astype(jnp.float32)
        for piece in range(1, pieces):
            acc = acc + back[group * pieces + piece].astype(jnp.float32)
        sums.append(acc)
    jobs = ((fwd_slots, fwd_gates, inputs, fwd_out, 0), (bwd_slots, bwd_gates, incoming, grad_out, cap))
    for slots, gates, block, out, first in jobs:
        total[:tokens] = block[...].astype(jnp.float32)
        for group in range(GROUPS):
            for slot in range(cap):
                row = pl.ds(slots[group * cap + slot], 1)
                piece = sums[group][first + slot : first + slot + 1]
                total[row] = total[row] + gates[group * cap + slot] * piece
        out[...] = total[:tokens].astype(out.dtype)


def settle(back, fwd_slots, fwd_gates, inputs, bwd_slots, bwd_gates, incoming):
    chips, both, width = back.shape
    tokens = inputs.shape[0]
    step = width // 4
    smem = pl.BlockSpec(memory_space=pltpu.SMEM)
    rows = pl.BlockSpec((tokens, step), lambda i: (0, i))
    return pl.pallas_call(
        settle_kernel,
        grid=(width // step,),
        out_shape=[jax.ShapeDtypeStruct((tokens, width), jnp.bfloat16)] * 2,
        in_specs=[smem] * 4 + [pl.BlockSpec((chips, both, step), lambda i: (0, 0, i)), rows, rows],
        out_specs=[rows, rows],
        scratch_shapes=[pltpu.VMEM((tokens + 8, step), jnp.float32)],
        compiler_params=pltpu.CompilerParams(vmem_limit_bytes=16 * 1024 * 1024),
        cost_estimate=pl.CostEstimate(flops=2 * chips * both * width, bytes_accessed=2560 * width // 4, transcendentals=0),
        name="settle",
    )(fwd_slots, fwd_gates, bwd_slots, bwd_gates, back, inputs, incoming)


def expert_kernel(rows, own, other, own_saved, other_saved, out, rows_in, lhs, weights, rows_sem, sems):
    chips, both, width = rows.shape
    count, piece = own_saved.shape[1:]
    parts = sems.shape[1]
    step = width // parts
    columns = [pl.ds(part * step, step) for part in range(parts)]
    rows_copy = pltpu.make_async_copy(rows, rows_in, rows_sem)
    rows_copy.start()
    copies = []
    for part in range(parts):
        for which, source in enumerate((own, other)):
            copy = pltpu.make_async_copy(
                source.at[:, columns[part]], weights.at[which, :, columns[part]], sems.at[which, part]
            )
            copy.start()
            copies.append(copy)
    rows_copy.wait()
    for chip in range(chips):
        lhs[pl.ds(chip * both, both)] = rows_in[chip].astype(jnp.float32)
    pre = [jnp.zeros((count, 3 * piece), jnp.float32) for _ in range(2)]
    for part in range(parts):
        left = lhs[:, columns[part]].astype(jnp.bfloat16)
        for which in range(2):
            copies[2 * part + which].wait()
            pre[which] = pre[which] + lax.dot_general(
                left,
                weights[which, :, columns[part]],
                (((1,), (1,)), ((), ())),
                preferred_element_type=jnp.float32,
            )
    is_fwd = lax.rem(lax.broadcasted_iota(jnp.int32, (count, piece), 0), both) < both // 2
    acts = []
    for which, saved in enumerate((own_saved, other_saved)):
        dh = pre[which][:, :piece]
        pre_gate = pre[which][:, piece : 2 * piece]
        pre_up = pre[which][:, 2 * piece :]
        hidden = jnp.where(is_fwd, jax.nn.silu(pre_gate) * pre_up, 0.0)
        pre_a = saved[0]
        pre_v = saved[1]
        sig = jax.nn.sigmoid(pre_a)
        slope = sig * (1.0 + pre_a * (1.0 - sig))
        d_gate = dh * pre_v * slope
        d_up = dh * (pre_a * sig)
        acts.append(jnp.concatenate([hidden, d_gate, d_up], axis=1).astype(jnp.bfloat16))
    for part in range(parts):
        total = jnp.dot(acts[0], weights[0, :, columns[part]], preferred_element_type=jnp.float32)
        total = total + jnp.dot(acts[1], weights[1, :, columns[part]], preferred_element_type=jnp.float32)
        for chip in range(chips):
            out[chip, :, columns[part]] = total[chip * both : (chip + 1) * both].astype(out.dtype)


def expert(rows, own, other, own_saved, other_saved):
    chips, both, width = rows.shape
    parts = 4
    vmem = pl.BlockSpec(memory_space=pltpu.VMEM)
    anywhere = pl.BlockSpec(memory_space=pl.ANY)
    return pl.pallas_call(
        expert_kernel,
        out_shape=jax.ShapeDtypeStruct(rows.shape, jnp.bfloat16),
        in_specs=[anywhere] * 3 + [vmem] * 2,
        out_specs=vmem,
        scratch_shapes=[
            pltpu.VMEM(rows.shape, jnp.bfloat16),
            pltpu.VMEM((chips * both, width), jnp.float32),
            pltpu.VMEM((2, *own.shape), jnp.bfloat16),
            pltpu.SemaphoreType.DMA,
            pltpu.SemaphoreType.DMA((2, parts)),
        ],
        compiler_params=pltpu.CompilerParams(vmem_limit_bytes=24 * 1024 * 1024),
        cost_estimate=pl.CostEstimate(
            flops=8 * chips * both * own.size, bytes_accessed=4 * own.size, transcendentals=0
        ),
        name="expert",
    )(rows, own, other, own_saved, other_saved)


def local(
    fwd_held,
    saved_preact,
    grad_held,
    gate_weight,
    up_weight,
    down_weight,
    fwd_slots,
    fwd_gates,
    bwd_slots,
    bwd_gates,
):
    width = fwd_held.shape[2]
    cap = fwd_slots.shape[3]
    both = 2 * cap
    length = lax.axis_size("expert")
    chips = length // CORES
    same_core = [[chip * CORES + core for chip in range(chips)] for core in range(CORES)]
    core = lax.axis_index("expert") % CORES
    w_gate = gate_weight[0]
    w_up = up_weight[0]
    w_down = down_weight[0]
    hidden_width = w_down.shape[0]

    inputs = shifted(fwd_held, "section", 1)[0]
    incoming = shifted(grad_held, "section", -1)[0]
    fwd_index = fwd_slots.reshape(-1)
    bwd_index = bwd_slots.reshape(-1)

    fwd_rows = pick_rows(fwd_index, inputs)
    bwd_rows = pick_rows(bwd_index, incoming)
    rows = jnp.concatenate(
        [fwd_rows.reshape(GROUPS, cap, width), bwd_rows.reshape(GROUPS, cap, width)], axis=1
    )
    rows = jnp.broadcast_to(rows[:, None], (GROUPS, chips // GROUPS, both, width))
    rows = rows.reshape(chips, both, width)
    rows, w_gate, w_up, saved = lax.optimization_barrier((rows, w_gate, w_up, saved_preact[0]))
    rows = lax.all_to_all(rows, "expert", 0, 0, axis_index_groups=same_core, tiled=True)

    own = jnp.concatenate([w_down, w_gate.T, w_up.T], axis=0)
    other = swapped(own, "expert")
    saved = saved.reshape(chips, CORES, cap, 2, hidden_width)
    own_saved = lax.dynamic_index_in_dim(saved, core, 1, keepdims=False)
    other_saved = swapped(lax.dynamic_index_in_dim(saved, 1 - core, 1, keepdims=False), "expert")

    def in_row_order(saved):
        saved = jnp.concatenate([jnp.zeros_like(saved), saved], axis=1)
        return saved.transpose(2, 0, 1, 3).reshape(2, -1, hidden_width).astype(jnp.float32)

    part = expert(rows, own, other, in_row_order(own_saved), in_row_order(other_saved))
    part = lax.all_to_all(part, "expert", 0, 0, axis_index_groups=same_core, tiled=True)
    fwd_out, grad_out = settle(
        part, fwd_index, fwd_gates.reshape(-1), inputs, bwd_index, bwd_gates.reshape(-1), incoming
    )
    return (fwd_out[None], grad_out[None])


def solution(mesh):
    in_specs = (
        P("section", "expert", None),
        P("section", None, None, None, "expert"),
        P("section", "expert", None),
        P("section", None, "expert"),
        P("section", None, "expert"),
        P("section", "expert", None),
        P("section", "expert", None, None),
        P("section", "expert", None, None),
        P("section", "expert", None, None),
        P("section", "expert", None, None),
    )
    out_specs = (P("section", "expert", None), P("section", "expert", None))
    return jax.shard_map(local, mesh=mesh, in_specs=in_specs, out_specs=out_specs, check_vma=False)
```

```python
import jax
import jax.numpy as jnp
from jax import lax
from jax.experimental import pallas as pl
from jax.experimental.pallas import tpu as pltpu
from jax.sharding import PartitionSpec as P

CORES = 2
GROUPS = 3


def shifted(shard, axis, by):
    length = lax.axis_size(axis)
    return lax.ppermute(shard, axis, [(i, (i + by) % length) for i in range(length)])


def swapped(shard, axis):
    length = lax.axis_size(axis)
    return lax.ppermute(shard, axis, [(i, i ^ 1) for i in range(length)])


def pick_rows(slots, block):
    onehot = slots[:, None] == jnp.arange(block.shape[0], dtype=jnp.int32)[None, :]
    return jnp.dot(onehot.astype(jnp.bfloat16), block, preferred_element_type=jnp.float32).astype(
        jnp.bfloat16
    )


def settle_kernel(
    fwd_slots, fwd_gates, bwd_slots, bwd_gates, back, inputs, incoming, fwd_out, grad_out, total
):
    chips, both, _ = back.shape
    cap = both // 2
    pieces = chips // GROUPS
    tokens = inputs.shape[0]
    sums = []
    for group in range(GROUPS):
        acc = back[group * pieces].astype(jnp.float32)
        for piece in range(1, pieces):
            acc = acc + back[group * pieces + piece].astype(jnp.float32)
        sums.append(acc)
    jobs = ((fwd_slots, fwd_gates, inputs, fwd_out, 0), (bwd_slots, bwd_gates, incoming, grad_out, cap))
    for slots, gates, block, out, first in jobs:
        total[:tokens] = block[...].astype(jnp.float32)
        for group in range(GROUPS):
            for slot in range(cap):
                row = pl.ds(slots[group * cap + slot], 1)
                piece = sums[group][first + slot : first + slot + 1]
                total[row] = total[row] + gates[group * cap + slot] * piece
        out[...] = total[:tokens].astype(out.dtype)


def settle(back, fwd_slots, fwd_gates, inputs, bwd_slots, bwd_gates, incoming):
    chips, both, width = back.shape
    tokens = inputs.shape[0]
    step = width // 4
    smem = pl.BlockSpec(memory_space=pltpu.SMEM)
    rows = pl.BlockSpec((tokens, step), lambda i: (0, i))
    return pl.pallas_call(
        settle_kernel,
        grid=(width // step,),
        out_shape=[jax.ShapeDtypeStruct((tokens, width), jnp.bfloat16)] * 2,
        in_specs=[smem] * 4 + [pl.BlockSpec((chips, both, step), lambda i: (0, 0, i)), rows, rows],
        out_specs=[rows, rows],
        scratch_shapes=[pltpu.VMEM((tokens + 8, step), jnp.float32)],
        compiler_params=pltpu.CompilerParams(vmem_limit_bytes=16777216),
        cost_estimate=pl.CostEstimate(flops=2 * chips * both * width, bytes_accessed=2560 * width // 4, transcendentals=0),
        name="settle",
    )(fwd_slots, fwd_gates, bwd_slots, bwd_gates, back, inputs, incoming)


def expert_kernel(rows, own, other_down, other_gate, other_up, own_saved, other_saved, out, rows_in, lhs, weights, saved_in, out_ready, rows_sem, sems, saved_sems, out_sems):
    chips, both, width = rows.shape
    count, piece = own_saved.shape[1:]
    parts = sems.shape[1]
    step = width // parts
    columns = [pl.ds(part * step, step) for part in range(parts)]
    rows_copy = pltpu.make_async_copy(rows, rows_in, rows_sem)
    rows_copy.start()
    copies = []
    for part in range(parts):
        for first, source in ((0, own), (3, other_down), (4, other_gate), (5, other_up)):
            target = weights.at[pl.ds(first * piece, source.shape[0]), columns[part]]
            copy = pltpu.make_async_copy(source.at[:, columns[part]], target, sems.at[first, part])
            copy.start()
            copies.append(copy)
    saved_copies = []
    for which, source in enumerate((own_saved, other_saved)):
        copy = pltpu.make_async_copy(source, saved_in.at[which], saved_sems.at[which])
        copy.start()
        saved_copies.append(copy)
    rows_copy.wait()
    for chip in range(chips):
        lhs[pl.ds(chip * both, both)] = rows_in[chip].astype(jnp.float32)
    pre = jnp.zeros((count, 6 * piece), jnp.float32)
    for part in range(parts):
        left = lhs[:, columns[part]].astype(jnp.bfloat16)
        for copy in copies[4 * part : 4 * part + 4]:
            copy.wait()
        pre = pre + lax.dot_general(
            left,
            weights[:, columns[part]],
            (((1,), (1,)), ((), ())),
            preferred_element_type=jnp.float32,
        )
    is_fwd = lax.rem(lax.broadcasted_iota(jnp.int32, (count, piece), 0), both) < both // 2
    acts = []
    for which in range(2):
        saved_copies[which].wait()
        saved = saved_in[which]
        dh, pre_gate, pre_up = (
            pre[:, (3 * which + i) * piece : (3 * which + i + 1) * piece] for i in range(3)
        )
        hidden = jnp.where(is_fwd, jax.nn.silu(pre_gate) * pre_up, 0.0)
        pre_a = saved[0]
        pre_v = saved[1]
        sig = jax.nn.sigmoid(pre_a)
        slope = sig * (1.0 + pre_a * (1.0 - sig))
        d_gate = dh * pre_v * slope
        d_up = dh * (pre_a * sig)
        acts += [hidden, d_gate, d_up]
    acts = jnp.concatenate(acts, axis=1).astype(jnp.bfloat16)
    out_copies = []
    for part in range(parts):
        total = jnp.dot(acts, weights[:, columns[part]], preferred_element_type=jnp.float32)
        for chip in range(chips):
            out_ready[chip, :, columns[part]] = total[chip * both : (chip + 1) * both].astype(out.dtype)
        copy = pltpu.make_async_copy(
            out_ready.at[:, :, columns[part]], out.at[:, :, columns[part]], out_sems.at[part]
        )
        copy.start()
        out_copies.append(copy)
    for copy in out_copies:
        copy.wait()


def expert(rows, own, others, own_saved, other_saved):
    chips, both, width = rows.shape
    parts = 4
    anywhere = pl.BlockSpec(memory_space=pl.ANY)
    hbm = pl.BlockSpec(memory_space=pltpu.HBM)
    return pl.pallas_call(
        expert_kernel,
        out_shape=jax.ShapeDtypeStruct(rows.shape, jnp.bfloat16),
        in_specs=[anywhere] + [hbm] * 4 + [anywhere] * 2,
        out_specs=hbm,
        scratch_shapes=[
            pltpu.VMEM(rows.shape, jnp.bfloat16),
            pltpu.VMEM((chips * both, width), jnp.float32),
            pltpu.VMEM((2 * own.shape[0], width), jnp.bfloat16),
            pltpu.VMEM((2, *own_saved.shape), jnp.float32),
            pltpu.VMEM(rows.shape, jnp.bfloat16),
            pltpu.SemaphoreType.DMA,
            pltpu.SemaphoreType.DMA((6, parts)),
            pltpu.SemaphoreType.DMA((2,)),
            pltpu.SemaphoreType.DMA((parts,)),
        ],
        compiler_params=pltpu.CompilerParams(vmem_limit_bytes=62914560),
        cost_estimate=pl.CostEstimate(
            flops=8 * chips * both * own.size, bytes_accessed=4 * own.size, transcendentals=0
        ),
        name="expert",
    )(rows, own, *others, own_saved, other_saved)


def local(
    fwd_held,
    saved_preact,
    grad_held,
    gate_weight,
    up_weight,
    down_weight,
    fwd_slots,
    fwd_gates,
    bwd_slots,
    bwd_gates,
):
    width = fwd_held.shape[2]
    cap = fwd_slots.shape[3]
    both = 2 * cap
    length = lax.axis_size("expert")
    chips = length // CORES
    same_core = [[chip * CORES + core for chip in range(chips)] for core in range(CORES)]
    core = lax.axis_index("expert") % CORES
    w_gate = gate_weight[0]
    w_up = up_weight[0]
    w_down = down_weight[0]
    hidden_width = w_down.shape[0]

    inputs = shifted(fwd_held, "section", 1)[0]
    incoming = shifted(grad_held, "section", -1)[0]
    fwd_index = fwd_slots.reshape(-1)
    bwd_index = bwd_slots.reshape(-1)

    fwd_rows = pick_rows(fwd_index, inputs)
    bwd_rows = pick_rows(bwd_index, incoming)
    rows = jnp.concatenate(
        [fwd_rows.reshape(GROUPS, cap, width), bwd_rows.reshape(GROUPS, cap, width)], axis=1
    )
    rows = jnp.broadcast_to(rows[:, None], (GROUPS, chips // GROUPS, both, width))
    rows = rows.reshape(chips, both, width)
    rows, w_gate, w_up, saved = lax.optimization_barrier((rows, w_gate, w_up, saved_preact[0]))
    rows = lax.all_to_all(rows, "expert", 0, 0, axis_index_groups=same_core, tiled=True)

    own = jnp.concatenate([w_down, w_gate.T, w_up.T], axis=0)
    pieces = [swapped(piece, "expert") for piece in jnp.split(own, 3, axis=0)]
    saved = saved.reshape(chips, CORES, cap, 2, hidden_width)
    own_saved = lax.dynamic_index_in_dim(saved, core, 1, keepdims=False)
    other_saved = swapped(lax.dynamic_index_in_dim(saved, 1 - core, 1, keepdims=False), "expert")

    def in_row_order(saved):
        saved = jnp.concatenate([jnp.zeros_like(saved), saved], axis=1)
        return saved.transpose(2, 0, 1, 3).reshape(2, -1, hidden_width).astype(jnp.float32)

    part = expert(rows, own, pieces, in_row_order(own_saved), in_row_order(other_saved))
    part = lax.all_to_all(part, "expert", 0, 0, axis_index_groups=same_core, tiled=True)
    fwd_out, grad_out = settle(
        part, fwd_index, fwd_gates.reshape(-1), inputs, bwd_index, bwd_gates.reshape(-1), incoming
    )
    return (fwd_out[None], grad_out[None])


def solution(mesh):
    in_specs = (
        P("section", "expert", None),
        P("section", None, None, None, "expert"),
        P("section", "expert", None),
        P("section", None, "expert"),
        P("section", None, "expert"),
        P("section", "expert", None),
        P("section", "expert", None, None),
        P("section", "expert", None, None),
        P("section", "expert", None, None),
        P("section", "expert", None, None),
    )
    out_specs = (P("section", "expert", None), P("section", "expert", None))
    return jax.shard_map(local, mesh=mesh, in_specs=in_specs, out_specs=out_specs, check_vma=False)
```

```python
import jax
import jax.numpy as jnp
from jax import lax
from jax.experimental import pallas as pl
from jax.experimental.pallas import tpu as pltpu
from jax.sharding import PartitionSpec as P

CORES = 2
GROUPS = 3
AHEAD = 2


def shifted(shard, axis, by):
    length = lax.axis_size(axis)
    return lax.ppermute(shard, axis, [(i, (i + by) % length) for i in range(length)])


def swapped(shard, axis):
    length = lax.axis_size(axis)
    return lax.ppermute(shard, axis, [(i, i ^ 1) for i in range(length)])


def pick_rows(slots, block):
    onehot = slots[:, None] == jnp.arange(block.shape[0], dtype=jnp.int32)[None, :]
    return jnp.dot(onehot.astype(jnp.bfloat16), block, preferred_element_type=jnp.float32).astype(
        jnp.bfloat16
    )


def settle_kernel(
    fwd_slots, fwd_gates, bwd_slots, bwd_gates, back, inputs, incoming, fwd_out, grad_out, total
):
    chips, both, _ = back.shape
    cap = both // 2
    pieces = chips // GROUPS
    tokens = inputs.shape[0]
    sums = []
    for group in range(GROUPS):
        acc = back[group * pieces].astype(jnp.float32)
        for piece in range(1, pieces):
            acc = acc + back[group * pieces + piece].astype(jnp.float32)
        sums.append(acc)
    jobs = ((fwd_slots, fwd_gates, inputs, fwd_out, 0), (bwd_slots, bwd_gates, incoming, grad_out, cap))
    for slots, gates, block, out, first in jobs:
        total[:tokens] = block[...].astype(jnp.float32)
        for group in range(GROUPS):
            for slot in range(cap):
                row = pl.ds(slots[group * cap + slot], 1)
                piece = sums[group][first + slot : first + slot + 1]
                total[row] = total[row] + gates[group * cap + slot] * piece
        out[...] = total[:tokens].astype(out.dtype)


def settle(back, fwd_slots, fwd_gates, inputs, bwd_slots, bwd_gates, incoming):
    chips, both, width = back.shape
    tokens = inputs.shape[0]
    step = width // 4
    smem = pl.BlockSpec(memory_space=pltpu.SMEM)
    rows = pl.BlockSpec((tokens, step), lambda i: (0, i))
    return pl.pallas_call(
        settle_kernel,
        grid=(width // step,),
        out_shape=[jax.ShapeDtypeStruct((tokens, width), jnp.bfloat16)] * 2,
        in_specs=[smem] * 4 + [pl.BlockSpec((chips, both, step), lambda i: (0, 0, i)), rows, rows],
        out_specs=[rows, rows],
        scratch_shapes=[pltpu.VMEM((tokens + 8, step), jnp.float32)],
        compiler_params=pltpu.CompilerParams(vmem_limit_bytes=16777216),
        cost_estimate=pl.CostEstimate(flops=2 * chips * both * width, bytes_accessed=2560 * width // 4, transcendentals=0),
        name="settle",
    )(fwd_slots, fwd_gates, bwd_slots, bwd_gates, back, inputs, incoming)


def expert_kernel(rows, own, other_down, other_gate, other_up, own_saved, other_saved, out, rows_in, lhs, weights, saved_in, out_ready, rows_sem, sems, saved_sems, out_sems):
    chips, both, width = rows.shape
    count, piece = own_saved.shape[1:]
    parts = sems.shape[1]
    step = width // parts
    columns = [pl.ds(part * step, step) for part in range(parts)]
    rows_copy = pltpu.make_async_copy(rows, rows_in, rows_sem)
    rows_copy.start()
    copies = []
    for part in range(parts):
        for first, source in ((0, own), (3, other_down), (4, other_gate), (5, other_up)):
            target = weights.at[pl.ds(first * piece, source.shape[0]), columns[part]]
            copies.append(pltpu.make_async_copy(source.at[:, columns[part]], target, sems.at[first, part]))
    for copy in copies[: 4 * AHEAD]:
        copy.start()
    saved_copies = []
    for which, source in enumerate((own_saved, other_saved)):
        copy = pltpu.make_async_copy(source, saved_in.at[which], saved_sems.at[which])
        copy.start()
        saved_copies.append(copy)
    rows_copy.wait()
    for chip in range(chips):
        lhs[pl.ds(chip * both, both)] = rows_in[chip].astype(jnp.float32)
    pre = jnp.zeros((6 * piece, count), jnp.float32)
    for part in range(parts):
        left = lhs[:, columns[part]].astype(jnp.bfloat16)
        for copy in copies[4 * part : 4 * part + 4]:
            copy.wait()
        for copy in copies[4 * (part + AHEAD) : 4 * (part + AHEAD) + 4]:
            copy.start()
        pre = pre + lax.dot_general(
            weights[:, columns[part]],
            left,
            (((1,), (1,)), ((), ())),
            preferred_element_type=jnp.float32,
        )
    pre = pre.T
    is_fwd = lax.rem(lax.broadcasted_iota(jnp.int32, (count, piece), 0), both) < both // 2
    acts = []
    for which in range(2):
        saved_copies[which].wait()
        saved = saved_in[which]
        dh, pre_gate, pre_up = (
            pre[:, (3 * which + i) * piece : (3 * which + i + 1) * piece] for i in range(3)
        )
        hidden = jnp.where(is_fwd, jax.nn.silu(pre_gate) * pre_up, 0.0)
        pre_a = saved[0]
        pre_v = saved[1]
        sig = jax.nn.sigmoid(pre_a)
        slope = sig * (1.0 + pre_a * (1.0 - sig))
        d_gate = dh * pre_v * slope
        d_up = dh * (pre_a * sig)
        acts += [hidden, d_gate, d_up]
    acts = jnp.concatenate(acts, axis=1).astype(jnp.bfloat16)
    out_copies = []
    for part in range(parts):
        total = jnp.dot(acts, weights[:, columns[part]], preferred_element_type=jnp.float32)
        for chip in range(chips):
            out_ready[chip, :, columns[part]] = total[chip * both : (chip + 1) * both].astype(out.dtype)
        copy = pltpu.make_async_copy(
            out_ready.at[:, :, columns[part]], out.at[:, :, columns[part]], out_sems.at[part]
        )
        copy.start()
        out_copies.append(copy)
    for copy in out_copies:
        copy.wait()


def expert(rows, own, others, own_saved, other_saved):
    chips, both, width = rows.shape
    parts = 4
    anywhere = pl.BlockSpec(memory_space=pl.ANY)
    hbm = pl.BlockSpec(memory_space=pltpu.HBM)
    return pl.pallas_call(
        expert_kernel,
        out_shape=jax.ShapeDtypeStruct(rows.shape, jnp.bfloat16),
        in_specs=[anywhere] + [hbm] * 4 + [anywhere] * 2,
        out_specs=hbm,
        scratch_shapes=[
            pltpu.VMEM(rows.shape, jnp.bfloat16),
            pltpu.VMEM((chips * both, width), jnp.float32),
            pltpu.VMEM((2 * own.shape[0], width), jnp.bfloat16),
            pltpu.VMEM((2, *own_saved.shape), jnp.float32),
            pltpu.VMEM(rows.shape, jnp.bfloat16),
            pltpu.SemaphoreType.DMA,
            pltpu.SemaphoreType.DMA((6, parts)),
            pltpu.SemaphoreType.DMA((2,)),
            pltpu.SemaphoreType.DMA((parts,)),
        ],
        compiler_params=pltpu.CompilerParams(vmem_limit_bytes=62914560),
        cost_estimate=pl.CostEstimate(
            flops=8 * chips * both * own.size, bytes_accessed=4 * own.size, transcendentals=0
        ),
        name="expert",
    )(rows, own, *others, own_saved, other_saved)


def local(
    fwd_held,
    saved_preact,
    grad_held,
    gate_weight,
    up_weight,
    down_weight,
    fwd_slots,
    fwd_gates,
    bwd_slots,
    bwd_gates,
):
    width = fwd_held.shape[2]
    cap = fwd_slots.shape[3]
    both = 2 * cap
    length = lax.axis_size("expert")
    chips = length // CORES
    same_core = [[chip * CORES + core for chip in range(chips)] for core in range(CORES)]
    core = lax.axis_index("expert") % CORES
    w_gate = gate_weight[0]
    w_up = up_weight[0]
    w_down = down_weight[0]
    hidden_width = w_down.shape[0]

    inputs = shifted(fwd_held, "section", 1)[0]
    incoming = shifted(grad_held, "section", -1)[0]
    fwd_index = fwd_slots.reshape(-1)
    bwd_index = bwd_slots.reshape(-1)

    fwd_rows = pick_rows(fwd_index, inputs)
    bwd_rows = pick_rows(bwd_index, incoming)
    rows = jnp.concatenate(
        [fwd_rows.reshape(GROUPS, cap, width), bwd_rows.reshape(GROUPS, cap, width)], axis=1
    )
    rows = jnp.broadcast_to(rows[:, None], (GROUPS, chips // GROUPS, both, width))
    rows = rows.reshape(chips, both, width)
    rows, w_gate, w_up, saved = lax.optimization_barrier((rows, w_gate, w_up, saved_preact[0]))
    rows = lax.all_to_all(rows, "expert", 0, 0, axis_index_groups=same_core, tiled=True)

    own = jnp.concatenate([w_down, w_gate.T, w_up.T], axis=0)
    pieces = [swapped(piece, "expert") for piece in jnp.split(own, 3, axis=0)]
    saved = saved.reshape(chips, CORES, cap, 2, hidden_width)
    own_saved = lax.dynamic_index_in_dim(saved, core, 1, keepdims=False)
    other_saved = swapped(lax.dynamic_index_in_dim(saved, 1 - core, 1, keepdims=False), "expert")

    def in_row_order(saved):
        saved = jnp.concatenate([jnp.zeros_like(saved), saved], axis=1)
        return saved.transpose(2, 0, 1, 3).reshape(2, -1, hidden_width).astype(jnp.float32)

    part = expert(rows, own, pieces, in_row_order(own_saved), in_row_order(other_saved))
    part = lax.all_to_all(part, "expert", 0, 0, axis_index_groups=same_core, tiled=True)
    fwd_out, grad_out = settle(
        part, fwd_index, fwd_gates.reshape(-1), inputs, bwd_index, bwd_gates.reshape(-1), incoming
    )
    return (fwd_out[None], grad_out[None])


def solution(mesh):
    in_specs = (
        P("section", "expert", None),
        P("section", None, None, None, "expert"),
        P("section", "expert", None),
        P("section", None, "expert"),
        P("section", None, "expert"),
        P("section", "expert", None),
        P("section", "expert", None, None),
        P("section", "expert", None, None),
        P("section", "expert", None, None),
        P("section", "expert", None, None),
    )
    out_specs = (P("section", "expert", None), P("section", "expert", None))
    return jax.shard_map(local, mesh=mesh, in_specs=in_specs, out_specs=out_specs, check_vma=False)
```

```python
import jax
import jax.numpy as jnp
from jax import lax
from jax.experimental import pallas as pl
from jax.experimental.pallas import tpu as pltpu
from jax.sharding import PartitionSpec as P

CORES = 2
GROUPS = 3
AHEAD = 2


def shifted(shard, axis, by):
    length = lax.axis_size(axis)
    return lax.ppermute(shard, axis, [(i, (i + by) % length) for i in range(length)])


def swapped(shard, axis):
    length = lax.axis_size(axis)
    return lax.ppermute(shard, axis, [(i, i ^ 1) for i in range(length)])


def pick_rows(slots, block):
    onehot = slots[:, None] == jnp.arange(block.shape[0], dtype=jnp.int32)[None, :]
    return jnp.dot(onehot.astype(jnp.bfloat16), block, preferred_element_type=jnp.float32).astype(
        jnp.bfloat16
    )


def settle_kernel(
    fwd_slots, fwd_gates, bwd_slots, bwd_gates, back, inputs, incoming, fwd_out, grad_out, total
):
    chips, both, _ = back.shape
    cap = both // 2
    pieces = chips // GROUPS
    tokens = inputs.shape[0]
    sums = []
    for group in range(GROUPS):
        acc = back[group * pieces].astype(jnp.float32)
        for piece in range(1, pieces):
            acc = acc + back[group * pieces + piece].astype(jnp.float32)
        sums.append(acc)
    jobs = ((fwd_slots, fwd_gates, inputs, fwd_out, 0), (bwd_slots, bwd_gates, incoming, grad_out, cap))
    for slots, gates, block, out, first in jobs:
        total[:tokens] = block[...].astype(jnp.float32)
        for group in range(GROUPS):
            for slot in range(cap):
                row = pl.ds(slots[group * cap + slot], 1)
                piece = sums[group][first + slot : first + slot + 1]
                total[row] = total[row] + gates[group * cap + slot] * piece
        out[...] = total[:tokens].astype(out.dtype)


def settle(back, fwd_slots, fwd_gates, inputs, bwd_slots, bwd_gates, incoming):
    chips, both, width = back.shape
    tokens = inputs.shape[0]
    step = width
    smem = pl.BlockSpec(memory_space=pltpu.SMEM)
    rows = pl.BlockSpec((tokens, step), lambda i: (0, i))
    return pl.pallas_call(
        settle_kernel,
        grid=(width // step,),
        out_shape=[jax.ShapeDtypeStruct((tokens, width), jnp.bfloat16)] * 2,
        in_specs=[smem] * 4 + [pl.BlockSpec((chips, both, step), lambda i: (0, 0, i)), rows, rows],
        out_specs=[rows, rows],
        scratch_shapes=[pltpu.VMEM((tokens + 8, step), jnp.float32)],
        compiler_params=pltpu.CompilerParams(vmem_limit_bytes=16777216),
        cost_estimate=pl.CostEstimate(flops=2 * chips * both * width, bytes_accessed=2560 * width // 4, transcendentals=0),
        name="settle",
    )(fwd_slots, fwd_gates, bwd_slots, bwd_gates, back, inputs, incoming)


def expert_kernel(rows, own, other_down, other_gate, other_up, own_saved, other_saved, out, rows_in, lhs, weights, saved_in, out_ready, rows_sem, sems, saved_sems, out_sems):
    chips, both, width = rows.shape
    count, piece = own_saved.shape[1:]
    parts = sems.shape[1]
    step = width // parts
    columns = [pl.ds(part * step, step) for part in range(parts)]
    rows_copy = pltpu.make_async_copy(rows, rows_in, rows_sem)
    rows_copy.start()
    copies = []
    for part in range(parts):
        for first, source in ((0, own), (3, other_down), (4, other_gate), (5, other_up)):
            target = weights.at[pl.ds(first * piece, source.shape[0]), columns[part]]
            copies.append(pltpu.make_async_copy(source.at[:, columns[part]], target, sems.at[first, part]))
    for copy in copies[: 4 * AHEAD]:
        copy.start()
    saved_copies = []
    for which, source in enumerate((own_saved, other_saved)):
        copy = pltpu.make_async_copy(source, saved_in.at[which], saved_sems.at[which])
        copy.start()
        saved_copies.append(copy)
    rows_copy.wait()
    for chip in range(chips):
        lhs[pl.ds(chip * both, both)] = rows_in[chip].astype(jnp.float32)
    pre = jnp.zeros((6 * piece, count), jnp.float32)
    for part in range(parts):
        left = lhs[:, columns[part]].astype(jnp.bfloat16)
        for copy in copies[4 * part : 4 * part + 4]:
            copy.wait()
        for copy in copies[4 * (part + AHEAD) : 4 * (part + AHEAD) + 4]:
            copy.start()
        pre = pre + lax.dot_general(
            weights[:, columns[part]],
            left,
            (((1,), (1,)), ((), ())),
            preferred_element_type=jnp.float32,
        )
    pre = pre.T
    is_fwd = lax.rem(lax.broadcasted_iota(jnp.int32, (count, piece), 0), both) < both // 2
    acts = []
    for which in range(2):
        saved_copies[which].wait()
        saved = saved_in[which]
        dh, pre_gate, pre_up = (
            pre[:, (3 * which + i) * piece : (3 * which + i + 1) * piece] for i in range(3)
        )
        hidden = jnp.where(is_fwd, jax.nn.silu(pre_gate) * pre_up, 0.0)
        pre_a = saved[0]
        pre_v = saved[1]
        sig = jax.nn.sigmoid(pre_a)
        slope = sig * (1.0 + pre_a * (1.0 - sig))
        d_gate = dh * pre_v * slope
        d_up = dh * (pre_a * sig)
        acts += [hidden, d_gate, d_up]
    acts = jnp.concatenate(acts, axis=1).astype(jnp.bfloat16)
    out_copies = []
    for part in range(parts):
        total = jnp.dot(acts, weights[:, columns[part]], preferred_element_type=jnp.float32)
        for chip in range(chips):
            out_ready[chip, :, columns[part]] = total[chip * both : (chip + 1) * both].astype(out.dtype)
        copy = pltpu.make_async_copy(
            out_ready.at[:, :, columns[part]], out.at[:, :, columns[part]], out_sems.at[part]
        )
        copy.start()
        out_copies.append(copy)
    for copy in out_copies:
        copy.wait()


def expert(rows, own, others, own_saved, other_saved):
    chips, both, width = rows.shape
    parts = 4
    anywhere = pl.BlockSpec(memory_space=pl.ANY)
    hbm = pl.BlockSpec(memory_space=pltpu.HBM)
    return pl.pallas_call(
        expert_kernel,
        out_shape=jax.ShapeDtypeStruct(rows.shape, jnp.bfloat16),
        in_specs=[anywhere] + [hbm] * 4 + [anywhere] * 2,
        out_specs=hbm,
        scratch_shapes=[
            pltpu.VMEM(rows.shape, jnp.bfloat16),
            pltpu.VMEM((chips * both, width), jnp.float32),
            pltpu.VMEM((2 * own.shape[0], width), jnp.bfloat16),
            pltpu.VMEM((2, *own_saved.shape), jnp.float32),
            pltpu.VMEM(rows.shape, jnp.bfloat16),
            pltpu.SemaphoreType.DMA,
            pltpu.SemaphoreType.DMA((6, parts)),
            pltpu.SemaphoreType.DMA((2,)),
            pltpu.SemaphoreType.DMA((parts,)),
        ],
        compiler_params=pltpu.CompilerParams(vmem_limit_bytes=62914560),
        cost_estimate=pl.CostEstimate(
            flops=8 * chips * both * own.size, bytes_accessed=4 * own.size, transcendentals=0
        ),
        name="expert",
    )(rows, own, *others, own_saved, other_saved)


def local(
    fwd_held,
    saved_preact,
    grad_held,
    gate_weight,
    up_weight,
    down_weight,
    fwd_slots,
    fwd_gates,
    bwd_slots,
    bwd_gates,
):
    width = fwd_held.shape[2]
    cap = fwd_slots.shape[3]
    both = 2 * cap
    length = lax.axis_size("expert")
    chips = length // CORES
    same_core = [[chip * CORES + core for chip in range(chips)] for core in range(CORES)]
    core = lax.axis_index("expert") % CORES
    w_gate = gate_weight[0]
    w_up = up_weight[0]
    w_down = down_weight[0]
    hidden_width = w_down.shape[0]

    inputs = shifted(fwd_held, "section", 1)[0]
    incoming = shifted(grad_held, "section", -1)[0]
    fwd_index = fwd_slots.reshape(-1)
    bwd_index = bwd_slots.reshape(-1)

    fwd_rows = pick_rows(fwd_index, inputs)
    bwd_rows = pick_rows(bwd_index, incoming)
    rows = jnp.concatenate(
        [fwd_rows.reshape(GROUPS, cap, width), bwd_rows.reshape(GROUPS, cap, width)], axis=1
    )
    rows = jnp.broadcast_to(rows[:, None], (GROUPS, chips // GROUPS, both, width))
    rows = rows.reshape(chips, both, width)
    rows, w_gate, w_up, saved = lax.optimization_barrier((rows, w_gate, w_up, saved_preact[0]))
    rows = lax.all_to_all(rows, "expert", 0, 0, axis_index_groups=same_core, tiled=True)

    own = jnp.concatenate([w_down, w_gate.T, w_up.T], axis=0)
    pieces = [swapped(piece, "expert") for piece in jnp.split(own, 3, axis=0)]
    saved = saved.reshape(chips, CORES, cap, 2, hidden_width)
    own_saved = lax.dynamic_index_in_dim(saved, core, 1, keepdims=False)
    other_saved = swapped(lax.dynamic_index_in_dim(saved, 1 - core, 1, keepdims=False), "expert")

    def in_row_order(saved):
        saved = jnp.concatenate([jnp.zeros_like(saved), saved], axis=1)
        return saved.transpose(2, 0, 1, 3).reshape(2, -1, hidden_width).astype(jnp.float32)

    part = expert(rows, own, pieces, in_row_order(own_saved), in_row_order(other_saved))
    part = lax.all_to_all(part, "expert", 0, 0, axis_index_groups=same_core, tiled=True)
    fwd_out, grad_out = settle(
        part, fwd_index, fwd_gates.reshape(-1), inputs, bwd_index, bwd_gates.reshape(-1), incoming
    )
    return (fwd_out[None], grad_out[None])


def solution(mesh):
    in_specs = (
        P("section", "expert", None),
        P("section", None, None, None, "expert"),
        P("section", "expert", None),
        P("section", None, "expert"),
        P("section", None, "expert"),
        P("section", "expert", None),
        P("section", "expert", None, None),
        P("section", "expert", None, None),
        P("section", "expert", None, None),
        P("section", "expert", None, None),
    )
    out_specs = (P("section", "expert", None), P("section", "expert", None))
    return jax.shard_map(local, mesh=mesh, in_specs=in_specs, out_specs=out_specs, check_vma=False)
```
